32 devices in a mesh: groups: 2 (over x), dp: 2 (over core), tensor: 8 (over z, y).
Axes of the slice: x: 2, y: 2, z: 4, core: 2. Of those that a mesh axis runs over, the one named last changes fastest.
Arguments:
- activations: bfloat16 [28672, 32768], P('tensor', ('groups', 'dp')), parts along dimension 1, may hold values from -6 to 6
- out_grads: bfloat16 [8192, 32768], P('tensor', ('groups', 'dp')), parts along dimension 1, may hold values from -6 to 6
- proj_in: bfloat16 [28672, 64], P('tensor'), may hold values from -0.03125 to 0.03125
- proj_out: bfloat16 [8192, 64], P('tensor'), may hold values from -0.0625 to 0.0625
- owners: int32 [16], P('groups'), parts along dimension 0, may hold values from 0 to 1, as said below
- valid_len: int32 [16], P(('groups', 'dp')), parts along dimension 0, may hold values from 256 to 2048
Outputs:
- logs: float32 [4, 4, 64, 64], P(('groups', 'dp'), None, 'tensor'), parts along dimension 0
The draws below stay inside these ranges and needn't reach their ends.
There are 2 independent parts, one for each index of `groups`. The reference program is written for one: setup_inputs(seed, part) draws one part's arguments, and reference() takes and returns one part's arrays. A program takes and returns all parts, laid end to end along the dimension named above; an argument that names none is the same for every part. Nothing has to cross between parts.
Inputs may be any that keep to these rules, and one draw needn't show every extreme that they name: `owners`: every shard number 0 to 2 - 1 is named by exactly 4 sequences.
All inputs are finite; a program needn't handle non-finite values.
Results may differ from the reference program's by a relative error of at most 0.0003.
Values sent between devices are 32-bit elements; how exact they have to be, the bound alone decides.
A program may use at most 192 MiB of HBM per device.

```python
import jax
import jax.numpy as jnp
from jax import lax

D = 8192
FF = 28672
RANK = 64
SEQ_LEN = 2048
SEQ_DEV = 4
EXAMPLES = 8
TOKENS = 16384
N_DP = 2


def draw_owners(key, part):
    key = jax.random.fold_in(key, 11)
    shuffled = jax.random.permutation(key, EXAMPLES)
    return (shuffled // SEQ_DEV).astype(jnp.int32)


def draw_valid_len(key, part):
    key = jax.random.fold_in(key, 23)
    first_key, second_key = jax.random.split(key)
    counts = jax.random.randint(first_key, (EXAMPLES,), SEQ_LEN // 8, SEQ_LEN + 1)
    chosen = jax.random.randint(second_key, (), 0, EXAMPLES)
    return jnp.where(jnp.arange(EXAMPLES) == chosen, SEQ_LEN, counts).astype(jnp.int32)


def levels(own_key, shape, cuts, low, largest):
    loudness = 1.0
    for position, parts in cuts:
        heights = jax.random.uniform(jax.random.fold_in(jax.random.fold_in(own_key, 6), position), (parts,), jnp.float32, low / len(cuts), largest / len(cuts))
        loudness = loudness * jnp.repeat(jnp.exp(heights), shape[position] // parts).reshape((-1,) + (1,) * (len(shape) - 1 - position))
    return loudness


def centred(stream_key, dims, scale, most, cuts=(), held_as=jnp.bfloat16):
    drawn = jax.random.normal(stream_key, dims, jnp.float32) * scale
    if len(cuts) > 0:
        drawn = levels(stream_key, dims, cuts, -0.22, 0.18) * drawn
    return jnp.clip(drawn, min=-most, max=most).astype(held_as)


def setup_inputs(seed: int = 0, part: int = 0) -> dict:
    splits = jax.random.split(jax.random.key(seed), 7)
    part_splits = jax.random.split(jax.random.fold_in(splits[6], part), 7)
    return {
        "activations": centred(part_splits[0], (FF, TOKENS), 1.0, 6.0, ((0, 8), (1, 2))),
        "out_grads": centred(part_splits[1], (D, TOKENS), 1.0, 6.0, ((0, 8), (1, 2))),
        "proj_in": centred(splits[2], (FF, RANK), FF ** -0.5, 0.03125, ((0, 8),)),
        "proj_out": centred(splits[3], (D, RANK), D ** -0.5, 0.0625, ((0, 8),)),
        "owners": draw_owners(jax.random.fold_in(jax.random.fold_in(splits[6], part), 71), part),
        "valid_len": draw_valid_len(jax.random.fold_in(jax.random.fold_in(splits[6], part), 71), part),
    }


def reference(activations, out_grads, proj_in, proj_out, owners, valid_len):
    act_proj = jnp.dot(proj_in.T, activations, preferred_element_type=jnp.float32)
    grad_proj = jnp.dot(proj_out.T, out_grads, preferred_element_type=jnp.float32)
    positions = jnp.arange(SEQ_LEN, dtype=jnp.int32)
    weights = (positions[None, :] < valid_len[:, None]).astype(jnp.float32)
    left_rows = act_proj.reshape(RANK, EXAMPLES, SEQ_LEN)
    right_rows = grad_proj.reshape(RANK, EXAMPLES, SEQ_LEN) * weights[None]
    grad_log = jnp.einsum('rel,qel->erq', left_rows, right_rows, precision=lax.Precision.HIGHEST)
    grad_log = grad_log / jnp.sqrt(valid_len.astype(jnp.float32))[:, None, None]
    grouped = jnp.argsort(owners, stable=True)
    return grad_log[grouped].reshape(N_DP, SEQ_DEV, RANK, RANK)
```

```python
import jax
import jax.numpy as jnp
from jax import lax
from jax.experimental import pallas as pl
from jax.experimental.pallas import tpu as pltpu
from jax.sharding import PartitionSpec as P

SEQ_LEN = 2048
MESH = pl.DeviceIdType.MESH
BLOCK = 512
SLOTS = 3
LAG_PAIR = 2
LAG_HOP = 1
LINE = 4
PAIR = 2


def project(weights, data):
    return lax.dot_general(
        weights, data, (((0,), (0,)), ((), ())), preferred_element_type=jnp.float32
    )


def fused(
    acts, grads, proj_in, proj_out, owners, valid_len, out,
    abuf, gbuf, win, wout, part, got_pair, got_up, got_down, prods, rows, got_rows,
    asem, gsem, pair_s, pair_r, up_s, up_r, down_s, down_r, row_s, row_r,
):
    dp = lax.axis_index("dp")
    me = lax.axis_index("tensor")
    z, y = me // PAIR, me % PAIR
    tensor = LINE * PAIR
    rank = proj_in.shape[1]
    blocks = acts.shape[1] // BLOCK
    per_seq = SEQ_LEN // BLOCK
    half = BLOCK // PAIR
    last = LINE - 1
    n_all = 2 * tensor
    lin = dp * tensor + me

    def fetch(b):
        slot = lax.rem(b, SLOTS)
        cols = pl.ds(pl.multiple_of(b * BLOCK, BLOCK), BLOCK)
        return (
            pltpu.make_async_copy(acts.at[:, cols], abuf.at[slot], asem.at[slot]),
            pltpu.make_async_copy(grads.at[:, cols], gbuf.at[slot], gsem.at[slot]),
        )

    for b in range(SLOTS):
        for copy in fetch(jnp.int32(b)):
            copy.start()

    barrier = pltpu.get_barrier_semaphore()
    for k in range(1, n_all):
        other = lax.rem(lin + k, n_all)
        pl.semaphore_signal(
            barrier, inc=1, device_id={"dp": other // tensor, "tensor": other % tensor},
            device_id_type=MESH,
        )
    win[...] = proj_in[...].astype(jnp.float32).T.astype(jnp.bfloat16)
    wout[...] = proj_out[...].astype(jnp.float32).T.astype(jnp.bfloat16)
    prods[...] = jnp.zeros_like(prods)
    pl.semaphore_wait(barrier, n_all - 1)

    def owner(j):
        return (3 * j) % LINE

    def pair_copy(j):
        return pltpu.make_async_remote_copy(
            src_ref=part.at[j, 1 - y], dst_ref=got_pair.at[j],
            send_sem=pair_s.at[j], recv_sem=pair_r.at[j],
            device_id={"tensor": z * PAIR + 1 - y}, device_id_type=MESH,
        )

    def up_copy(j, src):
        return pltpu.make_async_remote_copy(
            src_ref=src, dst_ref=got_up.at[j],
            send_sem=up_s.at[j], recv_sem=up_r.at[j],
            device_id={"tensor": (z + 1) * PAIR + y}, device_id_type=MESH,
        )

    def down_copy(j, src):
        return pltpu.make_async_remote_copy(
            src_ref=src, dst_ref=got_down.at[j],
            send_sem=down_s.at[j], recv_sem=down_r.at[j],
            device_id={"tensor": (z - 1) * PAIR + y}, device_id_type=MESH,
        )

    def step(b, carry):
        @pl.when(b < blocks)
        def _():
            slot = lax.rem(b, SLOTS)
            for copy in fetch(b):
                copy.wait()
            left = jnp.dot(win[...], abuf[slot], preferred_element_type=jnp.float32)
            right = jnp.dot(wout[...], gbuf[slot], preferred_element_type=jnp.float32)
            for h in range(PAIR):
                part[b, h, :rank, :] = left[:, h * half:(h + 1) * half]
                part[b, h, rank:, :] = right[:, h * half:(h + 1) * half]
            pair_copy(b).start()

            @pl.when(b + SLOTS < blocks)
            def _():
                for copy in fetch(b + SLOTS):
                    copy.start()

        j0 = b - LAG_PAIR

        @pl.when((j0 >= 0) & (j0 < blocks))
        def _():
            pair_copy(j0).wait()
            part[j0, y] = part[j0, y] + got_pair[j0]

            @pl.when((z == 0) & (owner(j0) > 0))
            def _():
                up_copy(j0, part.at[j0, y]).start()

            @pl.when((z == last) & (owner(j0) < last))
            def _():
                down_copy(j0, part.at[j0, y]).start()

        for dist in range(1, last):
            j = b - LAG_PAIR - dist * LAG_HOP
            inside = (j >= 0) & (j < blocks)

            @pl.when(inside & (z == dist) & (owner(j) > z))
            def _():
                copy = up_copy(j, got_up.at[j])
                copy.wait_recv()
                got_up[j] = got_up[j] + part[j, y]
                copy.start()

            @pl.when(inside & (z == last - dist) & (owner(j) < z))
            def _():
                copy = down_copy(j, got_down.at[j])
                copy.wait_recv()
                got_down[j] = got_down[j] + part[j, y]
                copy.start()

        j3 = b - LAG_PAIR - LAG_HOP * jnp.maximum(z, last - z)

        @pl.when((j3 >= 0) & (j3 < blocks) & (owner(j3) == z))
        def _():
            @pl.when(z > 0)
            def _():
                up_copy(j3, got_up.at[j3]).wait_recv()
                part[j3, y] = part[j3, y] + got_up[j3]

            @pl.when(z < last)
            def _():
                down_copy(j3, got_down.at[j3]).wait_recv()
                part[j3, y] = part[j3, y] + got_down[j3]

            seq = j3 // per_seq
            total = part[j3, y]
            first = (j3 % per_seq) * BLOCK + y * half
            place = first + lax.broadcasted_iota(jnp.int32, (rank, half), 1)
            a = total[:rank]
            g = jnp.where(place < valid_len[seq], total[rank:], 0.0)
            a_hi = a.astype(jnp.bfloat16)
            g_hi = g.astype(jnp.bfloat16)
            a_lo = (a - a_hi.astype(jnp.float32)).astype(jnp.bfloat16)
            g_lo = (g - g_hi.astype(jnp.float32)).astype(jnp.bfloat16)
            prods[seq] = prods[seq] + lax.dot_general(
                jnp.concatenate([a_hi, a_lo], 0), jnp.concatenate([g_hi, g_lo], 0),
                (((1,), (1,)), ((), ())), preferred_element_type=jnp.float32,
            )

        return carry

    lax.fori_loop(0, blocks + LAG_PAIR + LAG_HOP * last, step, 0)

    seqs = blocks // per_seq
    block_rows = rank // tensor
    for p in range(seqs // 2):
        halves = []
        for e in (2 * p, 2 * p + 1):
            q = prods[e]
            full = (
                q[rank:, rank:] + q[:rank, rank:] + q[rank:, :rank] + q[:rank, :rank]
            )
            length = jnp.full((rank, rank), valid_len[e], jnp.int32).astype(jnp.float32)
            halves.append(full / jnp.sqrt(length))
        both = jnp.concatenate(halves, 1)
        for r in range(tensor):
            rows[r, p] = both[r * block_rows:(r + 1) * block_rows]

    def row_copy(k):
        to = lax.rem(lin + k, n_all)
        return pltpu.make_async_remote_copy(
            src_ref=rows.at[to % tensor], dst_ref=got_rows.at[lin],
            send_sem=row_s.at[k], recv_sem=row_r.at[lin],
            device_id={"dp": to // tensor, "tensor": to % tensor}, device_id_type=MESH,
        )

    def row_arrival(k):
        source = lax.rem(lin + n_all - k, n_all)
        return pltpu.make_async_remote_copy(
            src_ref=rows.at[0], dst_ref=got_rows.at[source],
            send_sem=row_s.at[k], recv_sem=row_r.at[source],
            device_id={"dp": source // tensor, "tensor": source % tensor}, device_id_type=MESH,
        )

    for k in range(1, n_all):
        row_copy(k).start()
    got_rows[lin] = rows[me]

    def drain(j, carry):
        @pl.when((z < last) & (owner(j) > z))
        def _():
            up_copy(j, part.at[j, y]).wait_send()

        @pl.when((z > 0) & (owner(j) < z))
        def _():
            down_copy(j, part.at[j, y]).wait_send()

        return carry

    lax.fori_loop(0, blocks, drain, 0)
    for k in range(1, n_all):
        row_arrival(k).wait_recv()

    held = []
    for shard in range(2):
        total = got_rows[shard * tensor]
        for r in range(1, tensor):
            total = total + got_rows[shard * tensor + r]
        for e in range(seqs):
            held.append(total[e // 2][:, (e % 2) * rank:(e % 2 + 1) * rank])
    count = jnp.int32(0)
    places = [jnp.zeros_like(held[0])] * seqs
    for e, record in enumerate(held):
        mine = owners[e] == dp
        for s in range(seqs):
            share = jnp.where(mine & (count == s), 1.0, 0.0)
            places[s] = places[s] + share * record
        count = count + mine.astype(jnp.int32)
    for s in range(seqs):
        out[s] = places[s]
    for k in range(1, n_all):
        row_copy(k).wait_send()


def fused_local(acts, grads, proj_in, proj_out, owners, valid_len):
    rank = proj_in.shape[1]
    tokens = acts.shape[1]
    blocks = tokens // BLOCK
    half = BLOCK // PAIR
    seqs = tokens // SEQ_LEN
    tensor = LINE * PAIR
    block_rows = rank // tensor
    vmem = pl.BlockSpec(memory_space=pltpu.VMEM)
    smem = pl.BlockSpec(memory_space=pltpu.SMEM)
    anywhere = pl.BlockSpec(memory_space=pl.ANY)
    sems = pltpu.SemaphoreType.DMA
    stage = pltpu.VMEM((blocks, 2 * rank, half), jnp.float32)
    flops = 2 * rank * tokens * (acts.shape[0] + grads.shape[0])
    logs = pl.pallas_call(
        fused,
        out_shape=jax.ShapeDtypeStruct((seqs, block_rows, rank), jnp.float32),
        in_specs=[anywhere, anywhere, vmem, vmem, smem, smem],
        out_specs=vmem,
        scratch_shapes=[
            pltpu.VMEM((SLOTS, acts.shape[0], BLOCK), acts.dtype),
            pltpu.VMEM((SLOTS, grads.shape[0], BLOCK), grads.dtype),
            pltpu.VMEM((rank, acts.shape[0]), acts.dtype),
            pltpu.VMEM((rank, grads.shape[0]), grads.dtype),
            pltpu.VMEM((blocks, PAIR, 2 * rank, half), jnp.float32),
            stage, stage, stage,
            pltpu.VMEM((seqs, 2 * rank, 2 * rank), jnp.float32),
            pltpu.VMEM((tensor, seqs // 2, block_rows, 2 * rank), jnp.float32),
            pltpu.VMEM((2 * tensor, seqs // 2, block_rows, 2 * rank), jnp.float32),
            sems((SLOTS,)), sems((SLOTS,)),
            sems((blocks,)), sems((blocks,)),
            sems((blocks,)), sems((blocks,)),
            sems((blocks,)), sems((blocks,)),
            sems((2 * tensor,)), sems((2 * tensor,)),
        ],
        compiler_params=pltpu.CompilerParams(
            collective_id=0, has_side_effects=True, vmem_limit_bytes=48 * 2**20
        ),
        cost_estimate=pl.CostEstimate(
            flops=flops, bytes_accessed=2 * tokens * (acts.shape[0] + grads.shape[0]),
            transcendentals=0,
        ),
    )(acts, grads, proj_in, proj_out, owners, valid_len)
    return logs[None]


def local(activations, out_grads, proj_in, proj_out, owners, valid_len):
    rank_size = proj_in.shape[1]
    tokens = activations.shape[1]
    examples = tokens // SEQ_LEN
    shards = lax.axis_size("tensor")
    row_block = rank_size // shards
    my_index = lax.axis_index("tensor")
    grad_part = project(proj_out, out_grads)
    act_part = project(proj_in, activations)
    act_full, grad_full = lax.psum((act_part, grad_part), "tensor")
    act_rows = lax.dynamic_slice_in_dim(act_full, my_index * row_block, row_block, 0)
    positions = jnp.arange(SEQ_LEN, dtype=jnp.int32)
    weights = (positions[None, :] < valid_len[:, None]).astype(jnp.float32)
    left_rows = act_rows.reshape(row_block, examples, SEQ_LEN)
    right_rows = grad_full.reshape(rank_size, examples, SEQ_LEN) * weights[None]
    local_logs = jnp.einsum("rel,qel->erq", left_rows, right_rows, precision=lax.Precision.HIGHEST)
    local_logs = local_logs / jnp.sqrt(valid_len.astype(jnp.float32))[:, None, None]
    n_shards = lax.axis_size("dp")
    dp_index = lax.axis_index("dp")
    slot_ids = jnp.arange(examples, dtype=jnp.int32)
    my_owners = lax.dynamic_slice_in_dim(owners, dp_index * examples, examples, 0)
    targets = jnp.arange(n_shards, dtype=jnp.int32)
    matches = (my_owners[None, :] == targets[:, None]).astype(jnp.int32)
    slot_rank = jnp.cumsum(matches, axis=1) - matches
    packing = (matches[:, None, :] * (slot_rank[:, None, :] == slot_ids[None, :, None])).astype(
        jnp.float32
    )
    outgoing = jnp.einsum("oke,erq->okrq", packing, local_logs, precision=lax.Precision.HIGHEST)
    received = lax.all_to_all(outgoing, "dp", split_axis=0, concat_axis=0, tiled=True)
    owned_by_me = (owners.reshape(n_shards, examples) == dp_index).astype(jnp.int32)
    counts = jnp.sum(owned_by_me, axis=1)
    offsets = jnp.cumsum(counts) - counts
    valid_slot = slot_ids[None, :] < counts[:, None]
    target_pos = offsets[:, None] + slot_ids[None, :]
    placing = (valid_slot[None] & (target_pos[None] == slot_ids[:, None, None])).astype(jnp.float32)
    mine = jnp.einsum("psk,skrq->prq", placing, received, precision=lax.Precision.HIGHEST)
    return mine[None]


def solution(mesh):
    fits = mesh.shape["tensor"] == LINE * PAIR and mesh.shape["dp"] == 2
    return jax.shard_map(
        fused_local if fits else local,
        mesh=mesh,
        in_specs=(
            P("tensor", ("groups", "dp")),
            P("tensor", ("groups", "dp")),
            P("tensor", None),
            P("tensor", None),
            P("groups"),
            P(("groups", "dp")),
        ),
        out_specs=P(("groups", "dp"), None, "tensor", None),
        check_vma=False,
    )
```

```python
import jax
import jax.numpy as jnp
from jax import lax
from jax.experimental import pallas as pl
from jax.experimental.pallas import tpu as pltpu
from jax.sharding import PartitionSpec as P

SEQ_LEN = 2048
MESH = pl.DeviceIdType.MESH
BLOCK = 512
SLOTS = 3
QUARTERS = 4
LAG_PAIR = 4
LAG_HOP = 3
LAG_TWO = 3
LAG_LAST = 3
LINE = 4
PAIR = 2


def project(weights, data):
    return lax.dot_general(
        weights, data, (((0,), (0,)), ((), ())), preferred_element_type=jnp.float32
    )


def fused(
    acts, grads, win, wout, owners, valid_len, out,
    abuf, gbuf, part, got_pair, got_one, got_two, got_last, prods, rows, got_rows,
    asem, gsem, pair_s, pair_r, one_s, one_r, two_s, two_r, last_s, last_r, row_s, row_r,
):
    dp = lax.axis_index("dp")
    me = lax.axis_index("tensor")
    z, y = me // PAIR, me % PAIR
    tensor = LINE * PAIR
    rank = win.shape[0]
    blocks = acts.shape[1] // BLOCK
    per_seq = SEQ_LEN // BLOCK
    width = BLOCK // QUARTERS
    last = LINE - 1
    n_all = 2 * tensor
    lin = dp * tensor + me

    def fetch(b):
        slot = lax.rem(b, SLOTS)
        cols = pl.ds(pl.multiple_of(b * BLOCK, BLOCK), BLOCK)
        return (
            pltpu.make_async_copy(acts.at[:, cols], abuf.at[slot], asem.at[slot]),
            pltpu.make_async_copy(grads.at[:, cols], gbuf.at[slot], gsem.at[slot]),
        )

    for b in range(SLOTS):
        for copy in fetch(jnp.int32(b)):
            copy.start()

    barrier = pltpu.get_barrier_semaphore()
    for k in range(1, n_all):
        other = lax.rem(lin + k, n_all)
        pl.semaphore_signal(
            barrier, inc=1, device_id={"dp": other // tensor, "tensor": other % tensor},
            device_id_type=MESH,
        )
    prods[...] = jnp.zeros_like(prods)
    pl.semaphore_wait(barrier, n_all - 1)

    peer = z * PAIR + 1 - y

    def way_one(j):
        return 2 * (j % 2) - 1

    def way_two(j):
        return 1 - 2 * (j % 2)

    def begin(way):
        return last * (1 - way) // 2

    def end(way):
        return last * (1 + way) // 2

    def pair_copy(j):
        return pltpu.make_async_remote_copy(
            src_ref=part.at[j, 1 - y], dst_ref=got_pair.at[j],
            send_sem=pair_s.at[j], recv_sem=pair_r.at[j],
            device_id={"tensor": peer}, device_id_type=MESH,
        )

    def last_copy(j):
        return pltpu.make_async_remote_copy(
            src_ref=part.at[j, PAIR + 1 - y], dst_ref=got_last.at[j],
            send_sem=last_s.at[j], recv_sem=last_r.at[j],
            device_id={"tensor": peer}, device_id_type=MESH,
        )

    def one_copy(j, src):
        return pltpu.make_async_remote_copy(
            src_ref=src, dst_ref=got_one.at[j],
            send_sem=one_s.at[j], recv_sem=one_r.at[j],
            device_id={"tensor": (z + way_one(j)) * PAIR + y}, device_id_type=MESH,
        )

    def two_copy(j, src):
        return pltpu.make_async_remote_copy(
            src_ref=src, dst_ref=got_two.at[j],
            send_sem=two_s.at[j], recv_sem=two_r.at[j],
            device_id={"tensor": (z + way_two(j)) * PAIR + y}, device_id_type=MESH,
        )

    def both(j):
        return part.at[j, pl.ds(PAIR, PAIR)]

    def multiply(j, total, offset):
        seq = j // per_seq
        first = (j % per_seq) * BLOCK + offset
        place = first + lax.broadcasted_iota(jnp.int32, (rank, width), 1)
        a = total[:rank]
        g = jnp.where(place < valid_len[seq], total[rank:], 0.0)
        a_hi = a.astype(jnp.bfloat16)
        g_hi = g.astype(jnp.bfloat16)
        a_lo = (a - a_hi.astype(jnp.float32)).astype(jnp.bfloat16)
        g_lo = (g - g_hi.astype(jnp.float32)).astype(jnp.bfloat16)
        prods[seq] = prods[seq] + lax.dot_general(
            jnp.concatenate([a_hi, a_lo], 0), jnp.concatenate([g_hi, g_lo], 0),
            (((1,), (1,)), ((), ())), preferred_element_type=jnp.float32,
        )

    def step(b, carry):
        @pl.when(b < blocks)
        def _():
            slot = lax.rem(b, SLOTS)
            for copy in fetch(b):
                copy.wait()
            left = jnp.dot(win[...], abuf[slot], preferred_element_type=jnp.float32)
            right = jnp.dot(wout[...], gbuf[slot], preferred_element_type=jnp.float32)
            for h in range(QUARTERS):
                part[b, h, :rank, :] = left[:, h * width:(h + 1) * width]
                part[b, h, rank:, :] = right[:, h * width:(h + 1) * width]
            pair_copy(b).start()

            @pl.when(z == begin(way_two(b)))
            def _():
                two_copy(b, both(b)).start()

            @pl.when(b + SLOTS < blocks)
            def _():
                for copy in fetch(b + SLOTS):
                    copy.start()

        j0 = b - LAG_PAIR

        @pl.when((j0 >= 0) & (j0 < blocks))
        def _():
            pair_copy(j0).wait()
            part[j0, y] = part[j0, y] + got_pair[j0]

            @pl.when(z == begin(way_one(j0)))
            def _():
                one_copy(j0, part.at[j0, y]).start()

        for dist in range(1, last):
            j1 = b - LAG_PAIR - dist * LAG_HOP

            @pl.when((j1 >= 0) & (j1 < blocks) & (z == begin(way_one(j1)) + dist * way_one(j1)))
            def _():
                copy = one_copy(j1, got_one.at[j1])
                copy.wait_recv()
                got_one[j1] = got_one[j1] + part[j1, y]
                copy.start()

            j2 = b - dist * LAG_TWO

            @pl.when((j2 >= 0) & (j2 < blocks) & (z == begin(way_two(j2)) + dist * way_two(j2)))
            def _():
                copy = two_copy(j2, got_two.at[j2])
                copy.wait_recv()
                got_two[j2] = got_two[j2] + part[j2, PAIR:]
                copy.start()

        j3 = b - last * LAG_TWO

        @pl.when((j3 >= 0) & (j3 < blocks) & (z == end(way_two(j3))))
        def _():
            two_copy(j3, got_two.at[j3]).wait_recv()
            part[j3, PAIR:] = part[j3, PAIR:] + got_two[j3]
            last_copy(j3).start()

        j4 = b - LAG_PAIR - last * LAG_HOP

        @pl.when((j4 >= 0) & (j4 < blocks) & (z == end(way_one(j4))))
        def _():
            one_copy(j4, got_one.at[j4]).wait_recv()
            multiply(j4, part[j4, y] + got_one[j4], y * width)

        j5 = b - last * LAG_TWO - LAG_LAST

        @pl.when((j5 >= 0) & (j5 < blocks) & (z == end(way_two(j5))))
        def _():
            last_copy(j5).wait()
            multiply(j5, part[j5, PAIR + y] + got_last[j5], (PAIR + y) * width)

        return carry

    steps = blocks + max(LAG_PAIR + LAG_HOP * last, LAG_TWO * last + LAG_LAST)
    lax.fori_loop(0, steps, step, 0)

    seqs = blocks // per_seq
    block_rows = rank // tensor
    for p in range(seqs // 2):
        halves = []
        for e in (2 * p, 2 * p + 1):
            q = prods[e]
            full = (
                q[rank:, rank:] + q[:rank, rank:] + q[rank:, :rank] + q[:rank, :rank]
            )
            length = jnp.full((rank, rank), valid_len[e], jnp.int32).astype(jnp.float32)
            halves.append(full / jnp.sqrt(length))
        record = jnp.concatenate(halves, 1)
        for r in range(tensor):
            rows[r, p] = record[r * block_rows:(r + 1) * block_rows]

    def row_copy(k):
        to = lax.rem(lin + k, n_all)
        return pltpu.make_async_remote_copy(
            src_ref=rows.at[to % tensor], dst_ref=got_rows.at[lin],
            send_sem=row_s.at[k], recv_sem=row_r.at[lin],
            device_id={"dp": to // tensor, "tensor": to % tensor}, device_id_type=MESH,
        )

    def row_arrival(k):
        source = lax.rem(lin + n_all - k, n_all)
        return pltpu.make_async_remote_copy(
            src_ref=rows.at[0], dst_ref=got_rows.at[source],
            send_sem=row_s.at[k], recv_sem=row_r.at[source],
            device_id={"dp": source // tensor, "tensor": source % tensor}, device_id_type=MESH,
        )

    for k in range(1, n_all):
        row_copy(k).start()
    got_rows[lin] = rows[me]

    def drain(j, carry):
        @pl.when(z != end(way_one(j)))
        def _():
            one_copy(j, part.at[j, y]).wait_send()

        @pl.when(z != end(way_two(j)))
        def _():
            two_copy(j, both(j)).wait_send()

        return carry

    lax.fori_loop(0, blocks, drain, 0)
    for k in range(1, n_all):
        row_arrival(k).wait_recv()

    held = []
    for shard in range(2):
        total = got_rows[shard * tensor]
        for r in range(1, tensor):
            total = total + got_rows[shard * tensor + r]
        for e in range(seqs):
            held.append(total[e // 2][:, (e % 2) * rank:(e % 2 + 1) * rank])
    count = jnp.int32(0)
    places = [jnp.zeros_like(held[0])] * seqs
    for e, record in enumerate(held):
        mine = owners[e] == dp
        for s in range(seqs):
            share = jnp.where(mine & (count == s), 1.0, 0.0)
            places[s] = places[s] + share * record
        count = count + mine.astype(jnp.int32)
    for s in range(seqs):
        out[s] = places[s]
    for k in range(1, n_all):
        row_copy(k).wait_send()


def fused_local(acts, grads, proj_in, proj_out, owners, valid_len):
    rank = proj_in.shape[1]
    tokens = acts.shape[1]
    blocks = tokens // BLOCK
    width = BLOCK // QUARTERS
    seqs = tokens // SEQ_LEN
    tensor = LINE * PAIR
    block_rows = rank // tensor
    vmem = pl.BlockSpec(memory_space=pltpu.VMEM)
    smem = pl.BlockSpec(memory_space=pltpu.SMEM)
    anywhere = pl.BlockSpec(memory_space=pl.ANY)
    sems = pltpu.SemaphoreType.DMA
    stage = pltpu.VMEM((blocks, 2 * rank, width), jnp.float32)
    flops = 2 * rank * tokens * (acts.shape[0] + grads.shape[0])
    logs = pl.pallas_call(
        fused,
        out_shape=jax.ShapeDtypeStruct((seqs, block_rows, rank), jnp.float32),
        in_specs=[anywhere, anywhere, vmem, vmem, smem, smem],
        out_specs=vmem,
        scratch_shapes=[
            pltpu.VMEM((SLOTS, acts.shape[0], BLOCK), acts.dtype),
            pltpu.VMEM((SLOTS, grads.shape[0], BLOCK), grads.dtype),
            pltpu.VMEM((blocks, QUARTERS, 2 * rank, width), jnp.float32),
            stage, stage,
            pltpu.VMEM((blocks, PAIR, 2 * rank, width), jnp.float32),
            stage,
            pltpu.VMEM((seqs, 2 * rank, 2 * rank), jnp.float32),
            pltpu.VMEM((tensor, seqs // 2, block_rows, 2 * rank), jnp.float32),
            pltpu.VMEM((2 * tensor, seqs // 2, block_rows, 2 * rank), jnp.float32),
            sems((SLOTS,)), sems((SLOTS,)),
            sems((blocks,)), sems((blocks,)),
            sems((blocks,)), sems((blocks,)),
            sems((blocks,)), sems((blocks,)),
            sems((blocks,)), sems((blocks,)),
            sems((2 * tensor,)), sems((2 * tensor,)),
        ],
        compiler_params=pltpu.CompilerParams(
            collective_id=0, has_side_effects=True, vmem_limit_bytes=48 * 2**20
        ),
        cost_estimate=pl.CostEstimate(
            flops=flops, bytes_accessed=2 * tokens * (acts.shape[0] + grads.shape[0]),
            transcendentals=0,
        ),
    )(acts, grads, proj_in.T, proj_out.T, owners, valid_len)
    return logs[None]


def local(activations, out_grads, proj_in, proj_out, owners, valid_len):
    rank_size = proj_in.shape[1]
    tokens = activations.shape[1]
    examples = tokens // SEQ_LEN
    shards = lax.axis_size("tensor")
    row_block = rank_size // shards
    my_index = lax.axis_index("tensor")
    grad_part = project(proj_out, out_grads)
    act_part = project(proj_in, activations)
    act_full, grad_full = lax.psum((act_part, grad_part), "tensor")
    act_rows = lax.dynamic_slice_in_dim(act_full, my_index * row_block, row_block, 0)
    positions = jnp.arange(SEQ_LEN, dtype=jnp.int32)
    weights = (positions[None, :] < valid_len[:, None]).astype(jnp.float32)
    left_rows = act_rows.reshape(row_block, examples, SEQ_LEN)
    right_rows = grad_full.reshape(rank_size, examples, SEQ_LEN) * weights[None]
    local_logs = jnp.einsum("rel,qel->erq", left_rows, right_rows, precision=lax.Precision.HIGHEST)
    local_logs = local_logs / jnp.sqrt(valid_len.astype(jnp.float32))[:, None, None]
    n_shards = lax.axis_size("dp")
    dp_index = lax.axis_index("dp")
    slot_ids = jnp.arange(examples, dtype=jnp.int32)
    my_owners = lax.dynamic_slice_in_dim(owners, dp_index * examples, examples, 0)
    targets = jnp.arange(n_shards, dtype=jnp.int32)
    matches = (my_owners[None, :] == targets[:, None]).astype(jnp.int32)
    slot_rank = jnp.cumsum(matches, axis=1) - matches
    packing = (matches[:, None, :] * (slot_rank[:, None, :] == slot_ids[None, :, None])).astype(
        jnp.float32
    )
    outgoing = jnp.einsum("oke,erq->okrq", packing, local_logs, precision=lax.Precision.HIGHEST)
    received = lax.all_to_all(outgoing, "dp", split_axis=0, concat_axis=0, tiled=True)
    owned_by_me = (owners.reshape(n_shards, examples) == dp_index).astype(jnp.int32)
    counts = jnp.sum(owned_by_me, axis=1)
    offsets = jnp.cumsum(counts) - counts
    valid_slot = slot_ids[None, :] < counts[:, None]
    target_pos = offsets[:, None] + slot_ids[None, :]
    placing = (valid_slot[None] & (target_pos[None] == slot_ids[:, None, None])).astype(jnp.float32)
    mine = jnp.einsum("psk,skrq->prq", placing, received, precision=lax.Precision.HIGHEST)
    return mine[None]


def solution(mesh):
    fits = mesh.shape["tensor"] == LINE * PAIR and mesh.shape["dp"] == 2
    return jax.shard_map(
        fused_local if fits else local,
        mesh=mesh,
        in_specs=(
            P("tensor", ("groups", "dp")),
            P("tensor", ("groups", "dp")),
            P("tensor", None),
            P("tensor", None),
            P("groups"),
            P(("groups", "dp")),
        ),
        out_specs=P(("groups", "dp"), None, "tensor", None),
        check_vma=False,
    )
```

```python
import jax
import jax.numpy as jnp
from jax import lax
from jax.experimental import pallas as pl
from jax.experimental.pallas import tpu as pltpu
from jax.sharding import PartitionSpec as P

SEQ_LEN = 2048
MESH = pl.DeviceIdType.MESH
BLOCK = 512
SLOTS = 3
QUARTERS = 4
LAG_PAIR = 4
LAG_HOP = 3
LAG_TWO = 3
LAG_LAST = 3
LINE = 4
PAIR = 2


def project(weights, data):
    return lax.dot_general(
        weights, data, (((0,), (0,)), ((), ())), preferred_element_type=jnp.float32
    )


def fused(
    acts, grads, proj_in, proj_out, owners, valid_len, out,
    abuf, gbuf, win, wout, part, got_pair, got_one, got_two, got_last, prods, rows, got_rows,
    asem, gsem, pair_s, pair_r, one_s, one_r, two_s, two_r, last_s, last_r, row_s, row_r, wsem,
):
    dp = lax.axis_index("dp")
    me = lax.axis_index("tensor")
    z, y = me // PAIR, me % PAIR
    tensor = LINE * PAIR
    rank = win.shape[0]
    blocks = acts.shape[1] // BLOCK
    per_seq = SEQ_LEN // BLOCK
    width = BLOCK // QUARTERS
    last = LINE - 1
    n_all = 2 * tensor
    lin = dp * tensor + me

    def fetch(b):
        slot = lax.rem(b, SLOTS)
        cols = pl.ds(pl.multiple_of(b * BLOCK, BLOCK), BLOCK)
        return (
            pltpu.make_async_copy(acts.at[:, cols], abuf.at[slot], asem.at[slot]),
            pltpu.make_async_copy(grads.at[:, cols], gbuf.at[slot], gsem.at[slot]),
        )

    for b in range(SLOTS):
        for copy in fetch(jnp.int32(b)):
            copy.start()

    weights = (
        pltpu.make_async_copy(proj_in, win, wsem.at[0]),
        pltpu.make_async_copy(proj_out, wout, wsem.at[1]),
    )
    for copy in weights:
        copy.start()
    barrier = pltpu.get_barrier_semaphore()
    for k in range(1, n_all):
        other = lax.rem(lin + k, n_all)
        pl.semaphore_signal(
            barrier, inc=1, device_id={"dp": other // tensor, "tensor": other % tensor},
            device_id_type=MESH,
        )
    prods[...] = jnp.zeros_like(prods)
    pl.semaphore_wait(barrier, n_all - 1)
    for copy in weights:
        copy.wait()

    peer = z * PAIR + 1 - y

    def way_one(j):
        return 2 * (j % 2) - 1

    def way_two(j):
        return 1 - 2 * (j % 2)

    def begin(way):
        return last * (1 - way) // 2

    def end(way):
        return last * (1 + way) // 2

    def pair_copy(j):
        return pltpu.make_async_remote_copy(
            src_ref=part.at[j, 1 - y], dst_ref=got_pair.at[j],
            send_sem=pair_s.at[j], recv_sem=pair_r.at[j],
            device_id={"tensor": peer}, device_id_type=MESH,
        )

    def last_copy(j):
        return pltpu.make_async_remote_copy(
            src_ref=part.at[j, PAIR + 1 - y], dst_ref=got_last.at[j],
            send_sem=last_s.at[j], recv_sem=last_r.at[j],
            device_id={"tensor": peer}, device_id_type=MESH,
        )

    def one_copy(j, src):
        return pltpu.make_async_remote_copy(
            src_ref=src, dst_ref=got_one.at[j],
            send_sem=one_s.at[j], recv_sem=one_r.at[j],
            device_id={"tensor": (z + way_one(j)) * PAIR + y}, device_id_type=MESH,
        )

    def two_copy(j, src):
        return pltpu.make_async_remote_copy(
            src_ref=src, dst_ref=got_two.at[j],
            send_sem=two_s.at[j], recv_sem=two_r.at[j],
            device_id={"tensor": (z + way_two(j)) * PAIR + y}, device_id_type=MESH,
        )

    def both(j):
        return part.at[j, pl.ds(PAIR, PAIR)]

    def multiply(j, total, offset):
        seq = j // per_seq
        first = (j % per_seq) * BLOCK + offset
        place = first + lax.broadcasted_iota(jnp.int32, (rank, width), 1)
        a = total[:rank]
        g = jnp.where(place < valid_len[seq], total[rank:], 0.0)
        a_hi = a.astype(jnp.bfloat16)
        g_hi = g.astype(jnp.bfloat16)
        a_lo = (a - a_hi.astype(jnp.float32)).astype(jnp.bfloat16)
        g_lo = (g - g_hi.astype(jnp.float32)).astype(jnp.bfloat16)
        prods[seq] = prods[seq] + lax.dot_general(
            jnp.concatenate([a_hi, a_lo], 0), jnp.concatenate([g_hi, g_lo], 0),
            (((1,), (1,)), ((), ())), preferred_element_type=jnp.float32,
        )

    def step(b, carry):
        @pl.when(b < blocks)
        def _():
            slot = lax.rem(b, SLOTS)
            for copy in fetch(b):
                copy.wait()
            left = jnp.dot(win[...], abuf[slot], preferred_element_type=jnp.float32)
            right = jnp.dot(wout[...], gbuf[slot], preferred_element_type=jnp.float32)
            for h in range(QUARTERS):
                part[b, h, :rank, :] = left[:, h * width:(h + 1) * width]
                part[b, h, rank:, :] = right[:, h * width:(h + 1) * width]
            pair_copy(b).start()

            @pl.when(z == begin(way_two(b)))
            def _():
                two_copy(b, both(b)).start()

            @pl.when(b + SLOTS < blocks)
            def _():
                for copy in fetch(b + SLOTS):
                    copy.start()

        j0 = b - LAG_PAIR

        @pl.when((j0 >= 0) & (j0 < blocks))
        def _():
            pair_copy(j0).wait()
            part[j0, y] = part[j0, y] + got_pair[j0]

            @pl.when(z == begin(way_one(j0)))
            def _():
                one_copy(j0, part.at[j0, y]).start()

        for dist in range(1, last):
            j1 = b - LAG_PAIR - dist * LAG_HOP

            @pl.when((j1 >= 0) & (j1 < blocks) & (z == begin(way_one(j1)) + dist * way_one(j1)))
            def _():
                copy = one_copy(j1, got_one.at[j1])
                copy.wait_recv()
                got_one[j1] = got_one[j1] + part[j1, y]
                copy.start()

            j2 = b - dist * LAG_TWO

            @pl.when((j2 >= 0) & (j2 < blocks) & (z == begin(way_two(j2)) + dist * way_two(j2)))
            def _():
                copy = two_copy(j2, got_two.at[j2])
                copy.wait_recv()
                got_two[j2] = got_two[j2] + part[j2, PAIR:]
                copy.start()

        j3 = b - last * LAG_TWO

        @pl.when((j3 >= 0) & (j3 < blocks) & (z == end(way_two(j3))))
        def _():
            two_copy(j3, got_two.at[j3]).wait_recv()
            part[j3, PAIR:] = part[j3, PAIR:] + got_two[j3]
            last_copy(j3).start()

        j4 = b - LAG_PAIR - last * LAG_HOP

        @pl.when((j4 >= 0) & (j4 < blocks) & (z == end(way_one(j4))))
        def _():
            one_copy(j4, got_one.at[j4]).wait_recv()
            multiply(j4, part[j4, y] + got_one[j4], y * width)

        j5 = b - last * LAG_TWO - LAG_LAST

        @pl.when((j5 >= 0) & (j5 < blocks) & (z == end(way_two(j5))))
        def _():
            last_copy(j5).wait()
            multiply(j5, part[j5, PAIR + y] + got_last[j5], (PAIR + y) * width)

        return carry

    steps = blocks + max(LAG_PAIR + LAG_HOP * last, LAG_TWO * last + LAG_LAST)
    lax.fori_loop(0, steps, step, 0)

    seqs = blocks // per_seq
    block_rows = rank // tensor
    for p in range(seqs // 2):
        halves = []
        for e in (2 * p, 2 * p + 1):
            q = prods[e]
            full = (
                q[rank:, rank:] + q[:rank, rank:] + q[rank:, :rank] + q[:rank, :rank]
            )
            length = jnp.full((rank, rank), valid_len[e], jnp.int32).astype(jnp.float32)
            halves.append(full / jnp.sqrt(length))
        record = jnp.concatenate(halves, 1)
        for r in range(tensor):
            rows[r, p] = record[r * block_rows:(r + 1) * block_rows]

    def row_copy(k):
        to = lax.rem(lin + k, n_all)
        return pltpu.make_async_remote_copy(
            src_ref=rows.at[to % tensor], dst_ref=got_rows.at[lin],
            send_sem=row_s.at[k], recv_sem=row_r.at[lin],
            device_id={"dp": to // tensor, "tensor": to % tensor}, device_id_type=MESH,
        )

    def row_arrival(k):
        source = lax.rem(lin + n_all - k, n_all)
        return pltpu.make_async_remote_copy(
            src_ref=rows.at[0], dst_ref=got_rows.at[source],
            send_sem=row_s.at[k], recv_sem=row_r.at[source],
            device_id={"dp": source // tensor, "tensor": source % tensor}, device_id_type=MESH,
        )

    for k in range(1, n_all):
        row_copy(k).start()
    got_rows[lin] = rows[me]

    def drain(j, carry):
        @pl.when(z != end(way_one(j)))
        def _():
            one_copy(j, part.at[j, y]).wait_send()

        @pl.when(z != end(way_two(j)))
        def _():
            two_copy(j, both(j)).wait_send()

        return carry

    lax.fori_loop(0, blocks, drain, 0)
    for k in range(1, n_all):
        row_arrival(k).wait_recv()

    held = []
    for shard in range(2):
        total = got_rows[shard * tensor]
        for r in range(1, tensor):
            total = total + got_rows[shard * tensor + r]
        for e in range(seqs):
            held.append(total[e // 2][:, (e % 2) * rank:(e % 2 + 1) * rank])
    count = jnp.int32(0)
    places = [jnp.zeros_like(held[0])] * seqs
    for e, record in enumerate(held):
        mine = owners[e] == dp
        for s in range(seqs):
            share = jnp.where(mine & (count == s), 1.0, 0.0)
            places[s] = places[s] + share * record
        count = count + mine.astype(jnp.int32)
    for s in range(seqs):
        out[s] = places[s]
    for k in range(1, n_all):
        row_copy(k).wait_send()


def fused_local(acts, grads, proj_in, proj_out, owners, valid_len):
    rank = proj_in.shape[1]
    tokens = acts.shape[1]
    blocks = tokens // BLOCK
    width = BLOCK // QUARTERS
    seqs = tokens // SEQ_LEN
    tensor = LINE * PAIR
    block_rows = rank // tensor
    vmem = pl.BlockSpec(memory_space=pltpu.VMEM)
    smem = pl.BlockSpec(memory_space=pltpu.SMEM)
    anywhere = pl.BlockSpec(memory_space=pl.ANY)
    hbm = pl.BlockSpec(memory_space=pltpu.HBM)
    sems = pltpu.SemaphoreType.DMA
    stage = pltpu.VMEM((blocks, 2 * rank, width), jnp.float32)
    flops = 2 * rank * tokens * (acts.shape[0] + grads.shape[0])
    logs = pl.pallas_call(
        fused,
        out_shape=jax.ShapeDtypeStruct((seqs, block_rows, rank), jnp.float32),
        in_specs=[anywhere, anywhere, hbm, hbm, smem, smem],
        out_specs=vmem,
        scratch_shapes=[
            pltpu.VMEM((SLOTS, acts.shape[0], BLOCK), acts.dtype),
            pltpu.VMEM((SLOTS, grads.shape[0], BLOCK), grads.dtype),
            pltpu.VMEM((rank, acts.shape[0]), acts.dtype),
            pltpu.VMEM((rank, grads.shape[0]), grads.dtype),
            pltpu.VMEM((blocks, QUARTERS, 2 * rank, width), jnp.float32),
            stage, stage,
            pltpu.VMEM((blocks, PAIR, 2 * rank, width), jnp.float32),
            stage,
            pltpu.VMEM((seqs, 2 * rank, 2 * rank), jnp.float32),
            pltpu.VMEM((tensor, seqs // 2, block_rows, 2 * rank), jnp.float32),
            pltpu.VMEM((2 * tensor, seqs // 2, block_rows, 2 * rank), jnp.float32),
            sems((SLOTS,)), sems((SLOTS,)),
            sems((blocks,)), sems((blocks,)),
            sems((blocks,)), sems((blocks,)),
            sems((blocks,)), sems((blocks,)),
            sems((blocks,)), sems((blocks,)),
            sems((2 * tensor,)), sems((2 * tensor,)), sems((2,)),
        ],
        compiler_params=pltpu.CompilerParams(
            collective_id=0, has_side_effects=True, vmem_limit_bytes=48 * 2**20
        ),
        cost_estimate=pl.CostEstimate(
            flops=flops, bytes_accessed=2 * tokens * (acts.shape[0] + grads.shape[0]),
            transcendentals=0,
        ),
    )(acts, grads, proj_in.T, proj_out.T, owners, valid_len)
    return logs[None]


def local(activations, out_grads, proj_in, proj_out, owners, valid_len):
    rank_size = proj_in.shape[1]
    tokens = activations.shape[1]
    examples = tokens // SEQ_LEN
    shards = lax.axis_size("tensor")
    row_block = rank_size // shards
    my_index = lax.axis_index("tensor")
    grad_part = project(proj_out, out_grads)
    act_part = project(proj_in, activations)
    act_full, grad_full = lax.psum((act_part, grad_part), "tensor")
    act_rows = lax.dynamic_slice_in_dim(act_full, my_index * row_block, row_block, 0)
    positions = jnp.arange(SEQ_LEN, dtype=jnp.int32)
    weights = (positions[None, :] < valid_len[:, None]).astype(jnp.float32)
    left_rows = act_rows.reshape(row_block, examples, SEQ_LEN)
    right_rows = grad_full.reshape(rank_size, examples, SEQ_LEN) * weights[None]
    local_logs = jnp.einsum("rel,qel->erq", left_rows, right_rows, precision=lax.Precision.HIGHEST)
    local_logs = local_logs / jnp.sqrt(valid_len.astype(jnp.float32))[:, None, None]
    n_shards = lax.axis_size("dp")
    dp_index = lax.axis_index("dp")
    slot_ids = jnp.arange(examples, dtype=jnp.int32)
    my_owners = lax.dynamic_slice_in_dim(owners, dp_index * examples, examples, 0)
    targets = jnp.arange(n_shards, dtype=jnp.int32)
    matches = (my_owners[None, :] == targets[:, None]).astype(jnp.int32)
    slot_rank = jnp.cumsum(matches, axis=1) - matches
    packing = (matches[:, None, :] * (slot_rank[:, None, :] == slot_ids[None, :, None])).astype(
        jnp.float32
    )
    outgoing = jnp.einsum("oke,erq->okrq", packing, local_logs, precision=lax.Precision.HIGHEST)
    received = lax.all_to_all(outgoing, "dp", split_axis=0, concat_axis=0, tiled=True)
    owned_by_me = (owners.reshape(n_shards, examples) == dp_index).astype(jnp.int32)
    counts = jnp.sum(owned_by_me, axis=1)
    offsets = jnp.cumsum(counts) - counts
    valid_slot = slot_ids[None, :] < counts[:, None]
    target_pos = offsets[:, None] + slot_ids[None, :]
    placing = (valid_slot[None] & (target_pos[None] == slot_ids[:, None, None])).astype(jnp.float32)
    mine = jnp.einsum("psk,skrq->prq", placing, received, precision=lax.Precision.HIGHEST)
    return mine[None]


def solution(mesh):
    fits = mesh.shape["tensor"] == LINE * PAIR and mesh.shape["dp"] == 2
    return jax.shard_map(
        fused_local if fits else local,
        mesh=mesh,
        in_specs=(
            P("tensor", ("groups", "dp")),
            P("tensor", ("groups", "dp")),
            P("tensor", None),
            P("tensor", None),
            P("groups"),
            P(("groups", "dp")),
        ),
        out_specs=P(("groups", "dp"), None, "tensor", None),
        check_vma=False,
    )
```
